32 devices in a mesh: groups: 2 (over x), dap: 16 (over z, y, core).
Axes of the slice: x: 2, y: 2, z: 4, core: 2. Of those that a mesh axis runs over, the one named last changes fastest.
Arguments:
- pair_act: bfloat16 [64, 32, 128], P(('groups', 'dap')), parts along dimension 0, may hold values from -3 to 3
- chain_id: int32 [64], P('groups'), parts along dimension 0, may hold values from 0 to 3, as said below
- pad_mask: int32 [64], P('groups'), parts along dimension 0, may hold values from 0 to 1, as said below
- chain_table: float32 [2, 128], replicated, may hold values from -3 to 3
- out_project: bfloat16 [128, 512], replicated, may hold values from -0.5 to 0.5
- out_gate: bfloat16 [128, 128], replicated, may hold values from -0.5 to 0.5
- out_final: bfloat16 [128, 128], replicated, may hold values from -0.5 to 0.5
- in_project: bfloat16 [128, 512], replicated, may hold values from -0.5 to 0.5
- in_gate: bfloat16 [128, 128], replicated, may hold values from -0.5 to 0.5
- in_final: bfloat16 [128, 128], replicated, may hold values from -1 to 1
- start_project: bfloat16 [128, 512], replicated, may hold values from -0.5 to 0.5
- start_bias: bfloat16 [128, 4], replicated, may hold values from -1.75 to 1.75
- start_final: bfloat16 [128, 128], replicated, may hold values from -1.5 to 1.5
- end_project: bfloat16 [128, 512], replicated, may hold values from -0.5 to 0.5
- end_bias: bfloat16 [128, 4], replicated, may hold values from -1.75 to 1.75
- end_final: bfloat16 [128, 128], replicated, may hold values from -1.5 to 1.5
- trans_up: bfloat16 [128, 512], replicated, may hold values from -0.5 to 0.5
- trans_down: bfloat16 [512, 128], replicated, may hold values from -0.25 to 0.25
Outputs:
- pair_out: bfloat16 [64, 32, 128], P(('groups', 'dap')), parts along dimension 0
The draws below stay inside these ranges and needn't reach their ends.
There are 2 independent parts, one for each index of `groups`. The reference program is written for one: setup_inputs(seed, part) draws one part's arguments, and reference() takes and returns one part's arrays. A program takes and returns all parts, laid end to end along the dimension named above; an argument that names none is the same for every part. Nothing has to cross between parts.
Inputs may be any that keep to these rules, and one draw needn't show every extreme that they name: `chain_id`: chain numbers never fall along the residues; the first residue is in chain 0 and the last in chain 3. `pad_mask`: real residues (1) come first, padding (0) after; at least 16 residues are real and the last one is always padding.
All inputs are finite; a program needn't handle non-finite values.
Results may differ from the reference program's by a relative error of at most 0.025.
Values may be sent and summed in bfloat16 or wider, within the bound.
A program may use at most 64 MiB of HBM per device.

```python
import math
import jax
import jax.numpy as jnp
from jax import lax

C = 128
CH = 128
H = 4
HD = 32
TR = 512
L = 32


def draw_chain_id(key, part):
    key = jax.random.fold_in(key, 11)
    cuts = jax.random.randint(key, (3,), 1, L)
    positions = jnp.arange(L, dtype=jnp.int32)
    return jnp.sum((positions[:, None] >= cuts[None, :]).astype(jnp.int32), axis=1)


def draw_pad_mask(key, part):
    key = jax.random.fold_in(key, 23)
    live_count = jax.random.randint(key, (), L // 2, L)
    return (jnp.arange(L, dtype=jnp.int32) < live_count).astype(jnp.int32)


def block_levels(stream_key, dims, pieces, smallest, top_value):
    def one(position, shards_of):
        steps = jax.random.uniform(jax.random.fold_in(jax.random.fold_in(stream_key, 6), position), (shards_of,), jnp.float32, smallest / len(pieces), top_value / len(pieces))
        return jnp.repeat(jnp.exp(steps), dims[position] // shards_of).reshape((-1,) + (1,) * (len(dims) - position - 1))

    level = one(*pieces[0])
    for cut in pieces[1:]:
        level = level * one(*cut)
    return level


def noise(key, dims, scale, limit, pieces=(), kind=jnp.bfloat16):
    entries = scale * jax.random.normal(key, dims, jnp.float32)
    if pieces:
        entries = entries * block_levels(key, dims, pieces, -0.22, 0.18)
    return jnp.clip(entries, -limit, limit).astype(kind)


def setup_inputs(seed: int = 0, part: int = 0) -> dict:
    splits = jax.random.split(jax.random.key(seed), 19)
    part_keys = jax.random.split(jax.random.fold_in(splits[18], part), 19)
    return {
        "pair_act": noise(part_keys[0], (L, L, C), 0.5, 3.0, ((0, 16),)),
        "chain_id": draw_chain_id(jax.random.fold_in(jax.random.fold_in(splits[18], part), 71), part),
        "pad_mask": draw_pad_mask(jax.random.fold_in(jax.random.fold_in(splits[18], part), 71), part),
        "chain_table": noise(splits[3], (2, C), 0.5, 3.0, (), jnp.float32),
        "out_project": noise(splits[4], (C, 4 * CH), C ** -0.5, 0.5),
        "out_gate": noise(splits[5], (C, C), C ** -0.5, 0.5),
        "out_final": noise(splits[6], (CH, C), CH ** -0.5, 0.5),
        "in_project": noise(splits[7], (C, 4 * CH), C ** -0.5, 0.5),
        "in_gate": noise(splits[8], (C, C), C ** -0.5, 0.5),
        "in_final": noise(splits[9], (CH, C), (CH // 4) ** -0.5, 1.0),
        "start_project": noise(splits[10], (C, 4 * C), C ** -0.5, 0.5),
        "start_bias": noise(splits[11], (C, H), (C // 10) ** -0.5, 1.75),
        "start_final": noise(splits[12], (C, C), (C // 9) ** -0.5, 1.5),
        "end_project": noise(splits[13], (C, 4 * C), C ** -0.5, 0.5),
        "end_bias": noise(splits[14], (C, H), (C // 10) ** -0.5, 1.75),
        "end_final": noise(splits[15], (C, C), (C // 9) ** -0.5, 1.5),
        "trans_up": noise(splits[16], (C, TR), C ** -0.5, 0.5),
        "trans_down": noise(splits[17], (TR, C), TR ** -0.5, 0.25),
    }


epsilon = 1e-05
mask_scale = 1000000000.0

def layer_norm(values, along_axis):
    values = values.astype(jnp.float32)
    centred = values - lax.optimization_barrier(jnp.mean(values, axis=along_axis, keepdims=True))
    spread = lax.optimization_barrier(jnp.mean(centred * centred, axis=along_axis, keepdims=True))
    return centred * lax.rsqrt(spread + epsilon)

def by_rows(function, *members):
    total_rows = members[0].shape[0]
    block_rows = math.gcd(total_rows, 8)
    shaped = tuple((member.reshape((total_rows // block_rows, block_rows) + member.shape[1:]) for member in members))
    result = lax.map(lambda grouped: function(*grouped), shaped)
    return result.reshape((total_rows,) + result.shape[2:])

def mult_update(current, mask_all, weight_project, weight_gate, weight_final, outgoing):

    def project(rows_in, mask_rows):
        normed = layer_norm(rows_in, -1).astype(jnp.bfloat16)
        projected = jnp.einsum('ijc,ce->ije', normed.astype(jnp.float32), weight_project.astype(jnp.float32))
        pair_mask = (mask_rows[:, None] * mask_all[None, :])[:, :, None]
        left_side = (pair_mask * jax.nn.sigmoid(projected[..., CH:2 * CH]) * projected[..., :CH]).astype(jnp.bfloat16)
        right_side = (pair_mask * jax.nn.sigmoid(projected[..., 3 * CH:]) * projected[..., 2 * CH:3 * CH]).astype(jnp.bfloat16)
        return jnp.concatenate([left_side, right_side], axis=-1)
    both_sides = by_rows(project, current, mask_all)
    left_all = jnp.transpose(both_sides[..., :CH], (2, 0, 1))
    right_all = jnp.transpose(both_sides[..., CH:], (2, 0, 1))

    def channel(pair_sides):
        left_one, right_one = pair_sides
        if outgoing:
            product = jnp.dot(left_one, right_one.T, preferred_element_type=jnp.float32)
        else:
            product = jnp.dot(left_one.T, right_one, preferred_element_type=jnp.float32)
        return product.astype(jnp.bfloat16)
    combined = jnp.transpose(lax.map(channel, (left_all, right_all)), (1, 2, 0))

    def finish(rows_in, combined_rows):
        normed = layer_norm(rows_in, -1).astype(jnp.bfloat16)
        gate_full = jax.nn.sigmoid(jnp.einsum('ijc,cd->ijd', normed.astype(jnp.float32), weight_gate.astype(jnp.float32)))
        normed_out = layer_norm(combined_rows, -1).astype(jnp.bfloat16)
        update = jnp.einsum('ijc,cd->ijd', normed_out.astype(jnp.float32), weight_final.astype(jnp.float32))
        return (rows_in.astype(jnp.float32) + gate_full * update).astype(jnp.bfloat16)
    return by_rows(finish, current, combined)

def attend(current, mask_all, weight_project, weight_bias, weight_final):
    normed_all = by_rows(lambda rows_in: layer_norm(rows_in, -1).astype(jnp.bfloat16), current)
    bias_all = jnp.einsum('jkc,ch->hjk', normed_all.astype(jnp.float32), weight_bias.astype(jnp.float32)).astype(jnp.bfloat16)
    mask_bias = (mask_all - 1.0) * mask_scale
    scaling = 1.0 / math.sqrt(HD)

    def rows_update(normed):
        count_rows = normed.shape[0]
        projected = jnp.einsum('ijc,ce->ije', normed.astype(jnp.float32), weight_project.astype(jnp.float32))
        queries = projected[..., :C].astype(jnp.bfloat16).reshape(count_rows, L, H, HD)
        key_rows = projected[..., C:2 * C].astype(jnp.bfloat16).reshape(count_rows, L, H, HD)
        value_rows = projected[..., 2 * C:3 * C].astype(jnp.bfloat16).reshape(count_rows, L, H, HD)
        scores = jnp.einsum('ijhd,ikhd->ihjk', queries.astype(jnp.float32), key_rows.astype(jnp.float32)) * scaling
        scores = scores + bias_all.astype(jnp.float32)[None] + mask_bias[None, None, None, :]
        scores = scores - lax.optimization_barrier(jnp.max(scores, axis=-1, keepdims=True))
        expsum = jnp.exp(scores)
        weights = (expsum / lax.optimization_barrier(jnp.sum(expsum, axis=-1, keepdims=True))).astype(jnp.bfloat16)
        mixed = jnp.einsum('ihjk,ikhd->ijhd', weights.astype(jnp.float32), value_rows.astype(jnp.float32)).reshape(count_rows, L, C)
        gated = (mixed * jax.nn.sigmoid(projected[..., 3 * C:])).astype(jnp.bfloat16)
        return jnp.einsum('ijc,cd->ijd', gated.astype(jnp.float32), weight_final.astype(jnp.float32))
    return by_rows(rows_update, normed_all)

def reference(pair_act, chain_id, pad_mask, chain_table, out_project, out_gate, out_final, in_project, in_gate, in_final, start_project, start_bias, start_final, end_project, end_bias, end_final, trans_up, trans_down):
    mask_all = pad_mask.astype(jnp.float32)
    same_chain = chain_id[:, None] == chain_id[None, :]
    chain_add = jnp.where(same_chain[:, :, None], chain_table[1][None, None, :], chain_table[0][None, None, :])
    current = (pair_act.astype(jnp.float32) + chain_add).astype(jnp.bfloat16)
    current = mult_update(current, mask_all, out_project, out_gate, out_final, True)
    current = mult_update(current, mask_all, in_project, in_gate, in_final, False)
    start_update = attend(current, mask_all, start_project, start_bias, start_final)
    current = (current.astype(jnp.float32) + start_update).astype(jnp.bfloat16)
    end_update = attend(jnp.transpose(current, (1, 0, 2)), mask_all, end_project, end_bias, end_final)
    end_update = jnp.transpose(end_update.astype(jnp.bfloat16), (1, 0, 2))
    current = (current.astype(jnp.float32) + end_update.astype(jnp.float32)).astype(jnp.bfloat16)

    def transition(rows_in):
        normed = layer_norm(rows_in, -1).astype(jnp.bfloat16)
        hidden = jax.nn.relu(jnp.einsum('ijc,cf->ijf', normed.astype(jnp.float32), trans_up.astype(jnp.float32))).astype(jnp.bfloat16)
        update = jnp.einsum('ijf,fc->ijc', hidden.astype(jnp.float32), trans_down.astype(jnp.float32))
        return (rows_in.astype(jnp.float32) + update).astype(jnp.bfloat16)
    return by_rows(transition, current)
```

```python
import functools
import math

import jax
import jax.numpy as jnp
from jax import lax
from jax.experimental import pallas as pl
from jax.experimental.pallas import tpu as pltpu
from jax.sharding import PartitionSpec as P

epsilon = 1e-05
mask_scale = 1000000000.0


def layer_norm(values, along_axis):
    values = values.astype(jnp.float32)
    centred = values - jnp.mean(values, axis=along_axis, keepdims=True)
    spread = jnp.mean(centred * centred, axis=along_axis, keepdims=True)
    return centred * lax.rsqrt(spread + epsilon)


def regroup_second(values):
    return lax.all_to_all(values, "dap", split_axis=1, concat_axis=0, tiled=True)


def return_columns(values):
    return lax.all_to_all(values, "dap", split_axis=0, concat_axis=1, tiled=True)


def softmax_rows(scores):
    scores = scores - jnp.max(scores, axis=-1, keepdims=True)
    expsum = jnp.exp(scores)
    return (expsum / jnp.sum(expsum, axis=-1, keepdims=True)).astype(jnp.bfloat16)


def triangle_product(
    current, mask_rows, mask_all, weight_project, weight_gate, weight_final, outgoing
):
    hidden_width = weight_project.shape[1] // 4
    normed = layer_norm(current, -1).astype(jnp.bfloat16)
    projected = jnp.einsum(
        "ilc,ce->eil", normed, weight_project, preferred_element_type=jnp.float32
    )
    pair_mask = mask_rows[:, None] * mask_all[None, :]
    left_side = (
        pair_mask
        * jax.nn.sigmoid(projected[hidden_width : 2 * hidden_width])
        * projected[:hidden_width]
    ).astype(jnp.bfloat16)
    right_side = (
        pair_mask
        * jax.nn.sigmoid(projected[3 * hidden_width :])
        * projected[2 * hidden_width : 3 * hidden_width]
    ).astype(jnp.bfloat16)
    left_all, right_all = (
        lax.all_to_all(left_side, "dap", split_axis=0, concat_axis=1, tiled=True),
        lax.all_to_all(right_side, "dap", split_axis=0, concat_axis=1, tiled=True),
    )
    if outgoing:
        combined = jnp.einsum(
            "cik,cjk->cij", left_all, right_all, preferred_element_type=jnp.float32
        )
    else:
        combined = jnp.einsum(
            "cki,ckj->cij", left_all, right_all, preferred_element_type=jnp.float32
        )
    gathered = regroup_second(combined.astype(jnp.bfloat16))
    normed_out = layer_norm(gathered, 0).astype(jnp.bfloat16)
    update = jnp.einsum("cil,cd->ild", normed_out, weight_final, preferred_element_type=jnp.float32)
    gate_full = jax.nn.sigmoid(
        jnp.einsum("ilc,cd->ild", normed, weight_gate, preferred_element_type=jnp.float32)
    )
    return (current.astype(jnp.float32) + gate_full * update).astype(jnp.bfloat16)


def starting_node(current, mask_bias, weight_project, weight_bias, weight_final):
    row_count, length, width = current.shape
    heads = weight_bias.shape[1]
    head_dim = width // heads
    scaling = 1.0 / math.sqrt(head_dim)
    normed = layer_norm(current, -1).astype(jnp.bfloat16)
    projected = jnp.einsum(
        "ijc,ce->ije", normed, weight_project, preferred_element_type=jnp.float32
    )
    queries = (
        projected[..., :width].astype(jnp.bfloat16).reshape(row_count, length, heads, head_dim)
    )
    key_rows = (
        projected[..., width : 2 * width]
        .astype(jnp.bfloat16)
        .reshape(row_count, length, heads, head_dim)
    )
    value_rows = (
        projected[..., 2 * width : 3 * width]
        .astype(jnp.bfloat16)
        .reshape(row_count, length, heads, head_dim)
    )
    gate_values = jax.nn.sigmoid(projected[..., 3 * width :])
    bias_rows = jnp.einsum(
        "jkc,ch->jhk", normed, weight_bias, preferred_element_type=jnp.float32
    ).astype(jnp.bfloat16)
    piece_bias = lax.all_gather(bias_rows, "dap", axis=0, tiled=True)
    piece_rows = piece_bias.shape[0]
    block_rows = math.gcd(piece_rows, 64)

    def per_one_block(block_index):
        offset = block_index * block_rows
        bias_block = lax.dynamic_slice_in_dim(piece_bias, offset, block_rows, 0).astype(jnp.float32)
        query_block = lax.dynamic_slice_in_dim(queries, offset, block_rows, 1)
        scores = (
            jnp.einsum("ijhd,ikhd->ihjk", query_block, key_rows, preferred_element_type=jnp.float32)
            * scaling
        )
        scores = (
            scores + jnp.transpose(bias_block, (1, 0, 2))[None] + mask_bias[None, None, None, :]
        )
        weights = softmax_rows(scores)
        mixed_values = jnp.einsum(
            "ihjk,ikhd->ijhd", weights, value_rows, preferred_element_type=jnp.float32
        )
        mixed_values = mixed_values.reshape(row_count, block_rows, width)
        gate_block = lax.dynamic_slice_in_dim(gate_values, offset, block_rows, 1)
        return (mixed_values * gate_block).astype(jnp.bfloat16)

    blocks = lax.map(per_one_block, jnp.arange(piece_rows // block_rows, dtype=jnp.int32))
    attended = jnp.transpose(blocks, (1, 0, 2, 3)).reshape(row_count, piece_rows, width)
    update = jnp.einsum("ijc,cd->ijd", attended, weight_final, preferred_element_type=jnp.float32)
    return (current.astype(jnp.float32) + update).astype(jnp.bfloat16)


def transition(current, trans_up, trans_down):
    normed = layer_norm(current, -1).astype(jnp.bfloat16)
    hidden = jax.nn.relu(
        jnp.einsum("ijc,cf->ijf", normed, trans_up, preferred_element_type=jnp.float32)
    ).astype(jnp.bfloat16)
    update = jnp.einsum("ijf,fc->ijc", hidden, trans_down, preferred_element_type=jnp.float32)
    return (current.astype(jnp.float32) + update).astype(jnp.bfloat16)


def ending_node(
    current, mask_bias, weight_project, weight_bias, weight_final, trans_up, trans_down
):
    columns = regroup_second(current)
    length, col_count, width = columns.shape
    heads = weight_bias.shape[1]
    head_dim = width // heads
    scaling = 1.0 / math.sqrt(head_dim)
    normed = layer_norm(columns, -1).astype(jnp.bfloat16)
    projected = jnp.einsum(
        "ijc,ce->ije", normed, weight_project, preferred_element_type=jnp.float32
    )
    queries = (
        projected[..., :width].astype(jnp.bfloat16).reshape(length, col_count, heads, head_dim)
    )
    key_cols = (
        projected[..., width : 2 * width]
        .astype(jnp.bfloat16)
        .reshape(length, col_count, heads, head_dim)
    )
    value_cols = (
        projected[..., 2 * width : 3 * width]
        .astype(jnp.bfloat16)
        .reshape(length, col_count, heads, head_dim)
    )
    gate_values = jax.nn.sigmoid(projected[..., 3 * width :])
    own_normed = layer_norm(current, -1).astype(jnp.bfloat16)
    bias_part = jnp.einsum(
        "kic,ch->khi", own_normed, weight_bias, preferred_element_type=jnp.float32
    ).astype(jnp.bfloat16)

    def bias_slice(gathered, offset, block_rows):
        return jnp.transpose(lax.dynamic_slice_in_dim(gathered, offset, block_rows, 2), (1, 2, 0))

    gathered = lax.all_gather(bias_part, "dap", axis=0, tiled=True)
    block_rows = math.gcd(length, 64)

    def ending_one_block(block_index):
        offset = block_index * block_rows
        query_block = lax.dynamic_slice_in_dim(queries, offset, block_rows, 0)
        scores = (
            jnp.einsum("ijhd,kjhd->jhik", query_block, key_cols, preferred_element_type=jnp.float32)
            * scaling
        )
        scores = (
            scores
            + bias_slice(gathered, offset, block_rows).astype(jnp.float32)[None]
            + mask_bias[None, None, None, :]
        )
        weights = softmax_rows(scores)
        mixed_values = jnp.einsum(
            "jhik,kjhd->ijhd", weights, value_cols, preferred_element_type=jnp.float32
        )
        mixed_values = mixed_values.reshape(block_rows, col_count, width)
        gate_block = lax.dynamic_slice_in_dim(gate_values, offset, block_rows, 0)
        return (mixed_values * gate_block).astype(jnp.bfloat16)

    blocks = lax.map(ending_one_block, jnp.arange(length // block_rows, dtype=jnp.int32))
    attended = blocks.reshape(length, col_count, width)
    update = jnp.einsum(
        "ijc,cd->ijd", attended, weight_final, preferred_element_type=jnp.float32
    ).astype(jnp.bfloat16)
    columns = (columns.astype(jnp.float32) + update.astype(jnp.float32)).astype(jnp.bfloat16)
    finished = return_columns(transition(columns, trans_up, trans_down))
    return finished


def local(
    pair_act,
    chain_id,
    pad_mask,
    chain_table,
    out_project,
    out_gate,
    out_final,
    in_project,
    in_gate,
    in_final,
    start_project,
    start_bias,
    start_final,
    end_project,
    end_bias,
    end_final,
    trans_up,
    trans_down,
):
    row_count = pair_act.shape[0]
    first_row = lax.axis_index("dap") * row_count
    mask_all = pad_mask.astype(jnp.float32)
    mask_rows = lax.dynamic_slice_in_dim(mask_all, first_row, row_count, 0)
    chain_rows = lax.dynamic_slice_in_dim(chain_id, first_row, row_count, 0)
    same_chain = chain_rows[:, None] == chain_id[None, :]
    chain_add = jnp.where(
        same_chain[:, :, None], chain_table[1][None, None, :], chain_table[0][None, None, :]
    )
    current = (pair_act.astype(jnp.float32) + chain_add).astype(jnp.bfloat16)
    current = triangle_product(current, mask_rows, mask_all, out_project, out_gate, out_final, True)
    current = triangle_product(current, mask_rows, mask_all, in_project, in_gate, in_final, False)
    mask_bias = (mask_all - 1.0) * mask_scale
    current = starting_node(current, mask_bias, start_project, start_bias, start_final)
    return ending_node(current, mask_bias, end_project, end_bias, end_final, trans_up, trans_down)


def dot(left, right):
    return jnp.dot(left, right, preferred_element_type=jnp.float32)


def dot_rows(left, right):
    return lax.dot_general(
        left, right, (((1,), (1,)), ((), ())), preferred_element_type=jnp.float32
    )


def halves(values):
    high = values.astype(jnp.bfloat16)
    low = (values - high.astype(jnp.float32)).astype(jnp.bfloat16)
    return jnp.concatenate([high, low], axis=1)


def sigmoid(values):
    return 0.5 * jnp.tanh(0.5 * values) + 0.5


def norm_rows(values, average):
    width = values.shape[1]
    centred = values.astype(jnp.float32) - dot(values, average[:width])
    spread = dot(halves(centred * centred), average)
    return (centred * lax.rsqrt(spread + epsilon)).astype(jnp.bfloat16)


def fused_kernel(
    devices,
    pair_ref,
    chain_ref,
    mask_ref,
    table_ref,
    out_project_ref,
    out_gate_ref,
    out_final_ref,
    in_project_ref,
    in_gate_ref,
    in_final_ref,
    start_project_ref,
    start_bias_ref,
    start_final_ref,
    end_project_ref,
    end_bias_ref,
    end_final_ref,
    trans_up_ref,
    trans_down_ref,
    result_ref,
    pair_all,
    after_start,
    current,
    normed,
    left,
    right,
    key_all,
    value_all,
    chain_wide,
    mask_wide,
    start_scores,
    shift,
    own_rows,
    send_first,
    recv_first,
    send_second,
    recv_second,
):
    me = lax.axis_index("dap")
    block, width = pair_ref.shape
    length = chain_ref.shape[1]
    mine = block // length
    heads = start_bias_ref.shape[1]
    head_dim = width // heads
    scaling = 1.0 / math.sqrt(head_dim)
    tile = 8
    chunks = length // tile
    chunk_rows = tile * length
    f32, bf16 = jnp.float32, jnp.bfloat16

    barrier = pltpu.get_barrier_semaphore()
    for step in range(1, devices):
        peer = lax.rem(me + step, devices)
        pl.semaphore_signal(
            barrier, inc=1, device_id={"dap": peer}, device_id_type=pl.DeviceIdType.MESH
        )
    pl.semaphore_wait(barrier, devices - 1)

    my_block = pl.ds(pl.multiple_of(me * block, block), block)

    def exchange(source, target, send_sems, recv_sems):
        copies = []
        for step in range(1, devices):
            peer = lax.rem(me + step, devices)
            copies.append(
                pltpu.make_async_remote_copy(
                    src_ref=source,
                    dst_ref=target.at[my_block],
                    send_sem=send_sems.at[step],
                    recv_sem=recv_sems.at[step],
                    device_id={"dap": peer},
                    device_id_type=pl.DeviceIdType.MESH,
                )
            )
        for copy in copies:
            copy.start()
        return copies

    copies_first = exchange(pair_ref, pair_all, send_first, recv_first)
    pair_all[my_block, :] = pair_ref[...]

    average = jnp.full((2 * width, width), 1.0 / width, bf16)
    row_head = lax.broadcasted_iota(jnp.int32, (width, width), 0) // head_dim
    lane_head = lax.broadcasted_iota(jnp.int32, (width, width), 1) // head_dim
    same_head = jnp.where(row_head == lane_head, 1.0, 0.0).astype(bf16)
    same_head_twice = jnp.concatenate([same_head, same_head], axis=0)
    spread_heads = jnp.where(
        lax.broadcasted_iota(jnp.int32, (heads, width), 0)
        == lax.broadcasted_iota(jnp.int32, (heads, width), 1) // head_dim,
        1.0,
        0.0,
    ).astype(bf16)
    start_bias_wide = dot(start_bias_ref[...], spread_heads).astype(bf16)
    end_bias_wide = dot(end_bias_ref[...], spread_heads).astype(bf16)
    diagonal = lax.broadcasted_iota(jnp.int32, (length, length), 0) == lax.broadcasted_iota(
        jnp.int32, (length, length), 1
    )
    chain_column = jnp.sum(
        jnp.where(diagonal, chain_ref[...].astype(f32), 0.0), axis=1, keepdims=True
    )
    mask_column = jnp.sum(
        jnp.where(diagonal, mask_ref[...].astype(f32), 0.0), axis=1, keepdims=True
    )
    chain_wide[...] = jnp.broadcast_to(chain_column, (length, width))
    mask_all = jnp.broadcast_to(mask_column, (length, width))
    mask_wide[...] = mask_all
    key_lane = (
        lax.broadcasted_iota(jnp.int32, (length, width), 1) % length
        == lax.broadcasted_iota(jnp.int32, (length, width), 0)
    )
    mask_lanes = jnp.sum(jnp.where(key_lane, mask_all, 0.0), axis=0, keepdims=True)
    key_lane_ones = jnp.where(key_lane, 1.0, 0.0)

    for copy in copies_first:
        copy.wait_recv()

    def sides(chunk, normed_rows, weight_ref):
        projected = dot(normed_rows, weight_ref[...])
        rows_mask = mask_wide[pl.ds(chunk * tile, tile), :]
        pair_mask = jnp.concatenate(
            [mask_all * rows_mask[row : row + 1, :] for row in range(tile)], axis=0
        )
        left_side = pair_mask * sigmoid(projected[:, width : 2 * width]) * projected[:, :width]
        right_side = (
            pair_mask
            * sigmoid(projected[:, 3 * width :])
            * projected[:, 2 * width : 3 * width]
        )
        return left_side.astype(bf16).astype(f32), right_side.astype(bf16).astype(f32)

    def first(chunk, carry):
        rows = pl.ds(pl.multiple_of(chunk * chunk_rows, chunk_rows), chunk_rows)
        chain_rows = chain_wide[pl.ds(chunk * tile, tile), :]
        chain_all = chain_wide[...]
        within = table_ref[1:2, :]
        across = table_ref[0:1, :]
        added = jnp.concatenate(
            [
                jnp.where(chain_all == chain_rows[row : row + 1, :], within, across)
                for row in range(tile)
            ],
            axis=0,
        )
        start = (pair_all[rows, :].astype(f32) + added).astype(bf16)
        current[rows, :] = start
        rows_normed = norm_rows(start, average)
        normed[rows, :] = rows_normed
        left_side, right_side = sides(chunk, rows_normed, out_project_ref)
        left[rows, :] = left_side
        right[rows, :] = right_side
        return carry

    lax.fori_loop(0, chunks, first, 0)

    def finish(rows, combined, gate_ref, final_ref):
        combined_normed = norm_rows(combined.astype(bf16), average)
        update = dot(combined_normed, final_ref[...])
        gate = sigmoid(dot(normed[rows, :], gate_ref[...]))
        return (current[rows, :].astype(f32) + gate * update).astype(bf16)

    def outgoing(chunk, carry):
        rows = pl.ds(pl.multiple_of(chunk * chunk_rows, chunk_rows), chunk_rows)

        def add(step, totals):
            totals = list(totals)
            tiles = [
                left[pl.ds(pl.multiple_of((chunk * tile + row) * length + step * tile, tile), tile), :]
                for row in range(tile)
            ]
            for offset in range(tile):
                others = right[pl.ds(step * tile + offset, length, stride=length), :]
                for row in range(tile):
                    totals[row] = totals[row] + tiles[row][offset : offset + 1, :] * others
            return tuple(totals)

        totals = lax.fori_loop(
            0, chunks, add, tuple(jnp.zeros((length, width), f32) for _ in range(tile))
        )
        combined = jnp.concatenate(totals, axis=0)
        updated = finish(rows, combined, out_gate_ref, out_final_ref)
        current[rows, :] = updated
        return carry

    lax.fori_loop(0, chunks, outgoing, 0)

    def second(chunk, carry):
        rows = pl.ds(pl.multiple_of(chunk * chunk_rows, chunk_rows), chunk_rows)
        rows_normed = norm_rows(current[rows, :], average)
        normed[rows, :] = rows_normed
        left_side, right_side = sides(chunk, rows_normed, in_project_ref)
        left[rows, :] = left_side
        right[rows, :] = right_side
        return carry

    lax.fori_loop(0, chunks, second, 0)

    def incoming(chunk, carry):
        rows = pl.ds(pl.multiple_of(chunk * chunk_rows, chunk_rows), chunk_rows)

        def add(step, totals):
            totals = list(totals)
            for offset in range(tile):
                base = (step * tile + offset) * length
                own = left[pl.ds(pl.multiple_of(base + chunk * tile, tile), tile), :]
                others = right[pl.ds(pl.multiple_of(base, length), length), :]
                for row in range(tile):
                    totals[row] = totals[row] + own[row : row + 1, :] * others
            return tuple(totals)

        totals = lax.fori_loop(
            0, chunks, add, tuple(jnp.zeros((length, width), f32) for _ in range(tile))
        )
        combined = jnp.concatenate(totals, axis=0)
        updated = finish(rows, combined, in_gate_ref, in_final_ref)
        current[rows, :] = updated
        rows_normed = norm_rows(updated, average)
        bias = dot(rows_normed, start_bias_wide)
        bias = jnp.concatenate(
            [
                jnp.sum(
                    bias[row * length : (row + 1) * length, :] * key_lane_ones,
                    axis=0,
                    keepdims=True,
                )
                for row in range(tile)
            ],
            axis=0,
        )
        start_scores[pl.ds(pl.multiple_of(chunk * tile, tile), tile), :] = bias.astype(
            bf16
        ).astype(f32)
        return carry

    lax.fori_loop(0, chunks, incoming, 0)

    before = current[my_block, :]
    projected = dot(norm_rows(before, average), start_project_ref[...])
    gates = sigmoid(projected[:, 3 * width :])
    shared = start_scores[...] + (mask_lanes - 1.0) * mask_scale
    lane_of_head = lax.broadcasted_iota(jnp.int32, (length, width), 1) // length
    attended = []
    for row in range(mine):
        rows = slice(row * length, (row + 1) * length)
        queries = projected[rows, :width].astype(bf16)
        keys = projected[rows, width : 2 * width].astype(bf16)
        values = projected[rows, 2 * width : 3 * width].astype(bf16)
        keys = jnp.concatenate([keys] * heads, axis=0) * same_head
        values = jnp.concatenate([values] * heads, axis=0) * same_head
        scores = dot_rows(queries, keys) * scaling + shared
        top = jnp.zeros_like(scores)
        for head in range(heads):
            own_lanes = lane_of_head == head
            peak = jnp.max(jnp.where(own_lanes, scores, -jnp.inf), axis=1, keepdims=True)
            top = jnp.where(own_lanes, peak, top)
        weights = jnp.exp(scores - top)
        total = dot(halves(weights), same_head_twice)
        weights = (weights / total).astype(bf16)
        attended.append((dot(weights, values) * gates[rows, :]).astype(bf16))
    update = dot(jnp.concatenate(attended, axis=0), start_final_ref[...])
    own_rows[...] = (before.astype(f32) + update).astype(bf16)

    copies_second = exchange(own_rows, after_start, send_second, recv_second)
    own = own_rows[...]
    after_start[my_block, :] = own
    own_projected = dot(norm_rows(own, average), end_project_ref[...])
    for copy in copies_second:
        copy.wait_recv()

    def columns(chunk, carry):
        rows = pl.ds(pl.multiple_of(chunk * chunk_rows, chunk_rows), chunk_rows)
        rows_normed = norm_rows(after_start[rows, :], average)
        projected = dot(rows_normed, end_project_ref[:, width : 3 * width])
        key_all[rows, :] = projected[:, :width].astype(bf16).astype(f32)
        value_all[rows, :] = projected[:, width:].astype(bf16).astype(f32)
        left[rows, :] = dot(rows_normed, end_bias_wide).astype(bf16).astype(f32)
        return carry

    lax.fori_loop(0, chunks, columns, 0)
    gates = sigmoid(own_projected[:, 3 * width :])
    attended = []
    for row in range(mine):
        rows = slice(row * length, (row + 1) * length)
        queries = own_projected[rows, :width].astype(bf16).astype(f32)
        shared = left[pl.ds(me * mine + row, length, stride=length), :] + (
            mask_all - 1.0
        ) * mask_scale
        shift[...] = shared
        queries = jnp.concatenate([queries] * tile, axis=0)

        def score(step, top):
            rows = pl.ds(pl.multiple_of(step * chunk_rows, chunk_rows), chunk_rows)
            products = queries * key_all[rows, :]
            scores = dot(halves(products), same_head_twice) * scaling
            shifts = shift[pl.ds(pl.multiple_of(step * tile, tile), tile), :]
            for part in range(tile):
                piece = scores[part * length : (part + 1) * length, :] + shifts[part : part + 1, :]
                top = jnp.maximum(top, piece)
                right[
                    pl.ds(pl.multiple_of(step * chunk_rows + part * length, length), length), :
                ] = piece
            return top

        top = lax.fori_loop(0, chunks, score, jnp.full((length, width), -jnp.inf, f32))

        def mix(step, totals):
            total, mixed = totals
            for part in range(tile):
                rows = pl.ds(pl.multiple_of(step * chunk_rows + part * length, length), length)
                weights = jnp.exp(right[rows, :] - top)
                total = total + weights
                mixed = mixed + weights * value_all[rows, :]
            return total, mixed

        zero = jnp.zeros((length, width), f32)
        total, mixed = lax.fori_loop(0, chunks, mix, (zero, zero))
        attended.append((mixed / total * gates[slice(row * length, (row + 1) * length), :]).astype(bf16))
    update = dot(jnp.concatenate(attended, axis=0), end_final_ref[...]).astype(bf16)
    after_end = (own.astype(f32) + update.astype(f32)).astype(bf16)

    hidden = dot(norm_rows(after_end, average), trans_up_ref[...])
    hidden = jnp.maximum(hidden, 0.0).astype(bf16)
    update = dot(hidden, trans_down_ref[...])
    result_ref[...] = (after_end.astype(f32) + update).astype(bf16)

    for copy in copies_first + copies_second:
        copy.wait_send()


def fused(devices, pair_act, chain_id, pad_mask, *weights):
    mine, length, width = pair_act.shape
    block = mine * length
    pairs = length * length
    bf16, f32 = jnp.bfloat16, jnp.float32
    result = pl.pallas_call(
        functools.partial(fused_kernel, devices),
        out_shape=jax.ShapeDtypeStruct((block, width), bf16),
        in_specs=[pl.BlockSpec(memory_space=pltpu.VMEM)] * (3 + len(weights)),
        out_specs=pl.BlockSpec(memory_space=pltpu.VMEM),
        scratch_shapes=[
            pltpu.VMEM((pairs, width), bf16),
            pltpu.VMEM((pairs, width), bf16),
            pltpu.VMEM((pairs, width), bf16),
            pltpu.VMEM((pairs, width), bf16),
            pltpu.VMEM((pairs, width), f32),
            pltpu.VMEM((pairs, width), f32),
            pltpu.VMEM((pairs, width), f32),
            pltpu.VMEM((pairs, width), f32),
            pltpu.VMEM((length, width), f32),
            pltpu.VMEM((length, width), f32),
            pltpu.VMEM((length, width), f32),
            pltpu.VMEM((length, width), f32),
            pltpu.VMEM((block, width), bf16),
            pltpu.SemaphoreType.DMA((devices,)),
            pltpu.SemaphoreType.DMA((devices,)),
            pltpu.SemaphoreType.DMA((devices,)),
            pltpu.SemaphoreType.DMA((devices,)),
        ],
        compiler_params=pltpu.CompilerParams(
            collective_id=0, has_side_effects=True, vmem_limit_bytes=24 * 1024 * 1024
        ),
    )(
        pair_act.reshape(block, width),
        chain_id.reshape(1, length),
        pad_mask.reshape(1, length),
        *weights,
    )
    return result.reshape(mine, length, width)


def solution(mesh):
    devices = mesh.shape["dap"]

    def per_device(pair_act, chain_id, pad_mask, chain_table, *weights):
        mine, length, width = pair_act.shape
        heads = weights[7].shape[1]
        fits = (
            heads * length == width
            and width // heads == length
            and mine * devices == length
            and (mine * length) % 16 == 0
        )
        if fits:
            return fused(devices, pair_act, chain_id, pad_mask, chain_table, *weights)
        return local(pair_act, chain_id, pad_mask, chain_table, *weights)

    return jax.shard_map(
        per_device,
        mesh=mesh,
        in_specs=(
            P(("groups", "dap"), None, None),
            P("groups"),
            P("groups"),
            P(),
            P(),
            P(),
            P(),
            P(),
            P(),
            P(),
            P(),
            P(),
            P(),
            P(),
            P(),
            P(),
            P(),
            P(),
        ),
        out_specs=P(("groups", "dap"), None, None),
        check_vma=False,
    )
```

```python
import functools
import math

import jax
import jax.numpy as jnp
from jax import lax
from jax.experimental import pallas as pl
from jax.experimental.pallas import tpu as pltpu
from jax.sharding import PartitionSpec as P

epsilon = 1e-05
mask_scale = 1000000000.0


def layer_norm(values, along_axis):
    values = values.astype(jnp.float32)
    centred = values - jnp.mean(values, axis=along_axis, keepdims=True)
    spread = jnp.mean(centred * centred, axis=along_axis, keepdims=True)
    return centred * lax.rsqrt(spread + epsilon)


def regroup_second(values):
    return lax.all_to_all(values, "dap", split_axis=1, concat_axis=0, tiled=True)


def return_columns(values):
    return lax.all_to_all(values, "dap", split_axis=0, concat_axis=1, tiled=True)


def softmax_rows(scores):
    scores = scores - jnp.max(scores, axis=-1, keepdims=True)
    expsum = jnp.exp(scores)
    return (expsum / jnp.sum(expsum, axis=-1, keepdims=True)).astype(jnp.bfloat16)


def triangle_product(
    current, mask_rows, mask_all, weight_project, weight_gate, weight_final, outgoing
):
    hidden_width = weight_project.shape[1] // 4
    normed = layer_norm(current, -1).astype(jnp.bfloat16)
    projected = jnp.einsum(
        "ilc,ce->eil", normed, weight_project, preferred_element_type=jnp.float32
    )
    pair_mask = mask_rows[:, None] * mask_all[None, :]
    left_side = (
        pair_mask
        * jax.nn.sigmoid(projected[hidden_width : 2 * hidden_width])
        * projected[:hidden_width]
    ).astype(jnp.bfloat16)
    right_side = (
        pair_mask
        * jax.nn.sigmoid(projected[3 * hidden_width :])
        * projected[2 * hidden_width : 3 * hidden_width]
    ).astype(jnp.bfloat16)
    left_all, right_all = (
        lax.all_to_all(left_side, "dap", split_axis=0, concat_axis=1, tiled=True),
        lax.all_to_all(right_side, "dap", split_axis=0, concat_axis=1, tiled=True),
    )
    if outgoing:
        combined = jnp.einsum(
            "cik,cjk->cij", left_all, right_all, preferred_element_type=jnp.float32
        )
    else:
        combined = jnp.einsum(
            "cki,ckj->cij", left_all, right_all, preferred_element_type=jnp.float32
        )
    gathered = regroup_second(combined.astype(jnp.bfloat16))
    normed_out = layer_norm(gathered, 0).astype(jnp.bfloat16)
    update = jnp.einsum("cil,cd->ild", normed_out, weight_final, preferred_element_type=jnp.float32)
    gate_full = jax.nn.sigmoid(
        jnp.einsum("ilc,cd->ild", normed, weight_gate, preferred_element_type=jnp.float32)
    )
    return (current.astype(jnp.float32) + gate_full * update).astype(jnp.bfloat16)


def starting_node(current, mask_bias, weight_project, weight_bias, weight_final):
    row_count, length, width = current.shape
    heads = weight_bias.shape[1]
    head_dim = width // heads
    scaling = 1.0 / math.sqrt(head_dim)
    normed = layer_norm(current, -1).astype(jnp.bfloat16)
    projected = jnp.einsum(
        "ijc,ce->ije", normed, weight_project, preferred_element_type=jnp.float32
    )
    queries = (
        projected[..., :width].astype(jnp.bfloat16).reshape(row_count, length, heads, head_dim)
    )
    key_rows = (
        projected[..., width : 2 * width]
        .astype(jnp.bfloat16)
        .reshape(row_count, length, heads, head_dim)
    )
    value_rows = (
        projected[..., 2 * width : 3 * width]
        .astype(jnp.bfloat16)
        .reshape(row_count, length, heads, head_dim)
    )
    gate_values = jax.nn.sigmoid(projected[..., 3 * width :])
    bias_rows = jnp.einsum(
        "jkc,ch->jhk", normed, weight_bias, preferred_element_type=jnp.float32
    ).astype(jnp.bfloat16)
    piece_bias = lax.all_gather(bias_rows, "dap", axis=0, tiled=True)
    piece_rows = piece_bias.shape[0]
    block_rows = math.gcd(piece_rows, 64)

    def per_one_block(block_index):
        offset = block_index * block_rows
        bias_block = lax.dynamic_slice_in_dim(piece_bias, offset, block_rows, 0).astype(jnp.float32)
        query_block = lax.dynamic_slice_in_dim(queries, offset, block_rows, 1)
        scores = (
            jnp.einsum("ijhd,ikhd->ihjk", query_block, key_rows, preferred_element_type=jnp.float32)
            * scaling
        )
        scores = (
            scores + jnp.transpose(bias_block, (1, 0, 2))[None] + mask_bias[None, None, None, :]
        )
        weights = softmax_rows(scores)
        mixed_values = jnp.einsum(
            "ihjk,ikhd->ijhd", weights, value_rows, preferred_element_type=jnp.float32
        )
        mixed_values = mixed_values.reshape(row_count, block_rows, width)
        gate_block = lax.dynamic_slice_in_dim(gate_values, offset, block_rows, 1)
        return (mixed_values * gate_block).astype(jnp.bfloat16)

    blocks = lax.map(per_one_block, jnp.arange(piece_rows // block_rows, dtype=jnp.int32))
    attended = jnp.transpose(blocks, (1, 0, 2, 3)).reshape(row_count, piece_rows, width)
    update = jnp.einsum("ijc,cd->ijd", attended, weight_final, preferred_element_type=jnp.float32)
    return (current.astype(jnp.float32) + update).astype(jnp.bfloat16)


def transition(current, trans_up, trans_down):
    normed = layer_norm(current, -1).astype(jnp.bfloat16)
    hidden = jax.nn.relu(
        jnp.einsum("ijc,cf->ijf", normed, trans_up, preferred_element_type=jnp.float32)
    ).astype(jnp.bfloat16)
    update = jnp.einsum("ijf,fc->ijc", hidden, trans_down, preferred_element_type=jnp.float32)
    return (current.astype(jnp.float32) + update).astype(jnp.bfloat16)


def ending_node(
    current, mask_bias, weight_project, weight_bias, weight_final, trans_up, trans_down
):
    columns = regroup_second(current)
    length, col_count, width = columns.shape
    heads = weight_bias.shape[1]
    head_dim = width // heads
    scaling = 1.0 / math.sqrt(head_dim)
    normed = layer_norm(columns, -1).astype(jnp.bfloat16)
    projected = jnp.einsum(
        "ijc,ce->ije", normed, weight_project, preferred_element_type=jnp.float32
    )
    queries = (
        projected[..., :width].astype(jnp.bfloat16).reshape(length, col_count, heads, head_dim)
    )
    key_cols = (
        projected[..., width : 2 * width]
        .astype(jnp.bfloat16)
        .reshape(length, col_count, heads, head_dim)
    )
    value_cols = (
        projected[..., 2 * width : 3 * width]
        .astype(jnp.bfloat16)
        .reshape(length, col_count, heads, head_dim)
    )
    gate_values = jax.nn.sigmoid(projected[..., 3 * width :])
    own_normed = layer_norm(current, -1).astype(jnp.bfloat16)
    bias_part = jnp.einsum(
        "kic,ch->khi", own_normed, weight_bias, preferred_element_type=jnp.float32
    ).astype(jnp.bfloat16)

    def bias_slice(gathered, offset, block_rows):
        return jnp.transpose(lax.dynamic_slice_in_dim(gathered, offset, block_rows, 2), (1, 2, 0))

    gathered = lax.all_gather(bias_part, "dap", axis=0, tiled=True)
    block_rows = math.gcd(length, 64)

    def ending_one_block(block_index):
        offset = block_index * block_rows
        query_block = lax.dynamic_slice_in_dim(queries, offset, block_rows, 0)
        scores = (
            jnp.einsum("ijhd,kjhd->jhik", query_block, key_cols, preferred_element_type=jnp.float32)
            * scaling
        )
        scores = (
            scores
            + bias_slice(gathered, offset, block_rows).astype(jnp.float32)[None]
            + mask_bias[None, None, None, :]
        )
        weights = softmax_rows(scores)
        mixed_values = jnp.einsum(
            "jhik,kjhd->ijhd", weights, value_cols, preferred_element_type=jnp.float32
        )
        mixed_values = mixed_values.reshape(block_rows, col_count, width)
        gate_block = lax.dynamic_slice_in_dim(gate_values, offset, block_rows, 0)
        return (mixed_values * gate_block).astype(jnp.bfloat16)

    blocks = lax.map(ending_one_block, jnp.arange(length // block_rows, dtype=jnp.int32))
    attended = blocks.reshape(length, col_count, width)
    update = jnp.einsum(
        "ijc,cd->ijd", attended, weight_final, preferred_element_type=jnp.float32
    ).astype(jnp.bfloat16)
    columns = (columns.astype(jnp.float32) + update.astype(jnp.float32)).astype(jnp.bfloat16)
    finished = return_columns(transition(columns, trans_up, trans_down))
    return finished


def local(
    pair_act,
    chain_id,
    pad_mask,
    chain_table,
    out_project,
    out_gate,
    out_final,
    in_project,
    in_gate,
    in_final,
    start_project,
    start_bias,
    start_final,
    end_project,
    end_bias,
    end_final,
    trans_up,
    trans_down,
):
    row_count = pair_act.shape[0]
    first_row = lax.axis_index("dap") * row_count
    mask_all = pad_mask.astype(jnp.float32)
    mask_rows = lax.dynamic_slice_in_dim(mask_all, first_row, row_count, 0)
    chain_rows = lax.dynamic_slice_in_dim(chain_id, first_row, row_count, 0)
    same_chain = chain_rows[:, None] == chain_id[None, :]
    chain_add = jnp.where(
        same_chain[:, :, None], chain_table[1][None, None, :], chain_table[0][None, None, :]
    )
    current = (pair_act.astype(jnp.float32) + chain_add).astype(jnp.bfloat16)
    current = triangle_product(current, mask_rows, mask_all, out_project, out_gate, out_final, True)
    current = triangle_product(current, mask_rows, mask_all, in_project, in_gate, in_final, False)
    mask_bias = (mask_all - 1.0) * mask_scale
    current = starting_node(current, mask_bias, start_project, start_bias, start_final)
    return ending_node(current, mask_bias, end_project, end_bias, end_final, trans_up, trans_down)


def dot(left, right):
    return jnp.dot(left, right, preferred_element_type=jnp.float32)


def dot_rows(left, right):
    return lax.dot_general(
        left, right, (((1,), (1,)), ((), ())), preferred_element_type=jnp.float32
    )


def dot_columns(left, right):
    return lax.dot_general(
        left, right, (((0,), (0,)), ((), ())), preferred_element_type=jnp.float32
    )


def halves(values):
    high = values.astype(jnp.bfloat16)
    low = (values - high.astype(jnp.float32)).astype(jnp.bfloat16)
    return jnp.concatenate([high, low], axis=1)


def sigmoid(values):
    return 0.5 * jnp.tanh(0.5 * values) + 0.5


def norm_rows(values, average):
    width = values.shape[1]
    centred = values.astype(jnp.float32) - dot(values, average[:width])
    spread = dot(halves(centred * centred), average)
    return (centred * lax.rsqrt(spread + epsilon)).astype(jnp.bfloat16)


def fused_kernel(
    devices,
    count,
    *refs,
):
    sources, result_ref, held = refs[:count], refs[count], refs[count + 1 : 2 * count + 1]
    (
        pair_ref,
        chain_ref,
        mask_ref,
        table_ref,
        out_project_ref,
        out_gate_ref,
        out_final_ref,
        in_project_ref,
        in_gate_ref,
        in_final_ref,
        start_project_ref,
        start_bias_ref,
        start_final_ref,
        end_project_ref,
        end_bias_ref,
        end_final_ref,
        trans_up_ref,
        trans_down_ref,
    ) = held
    (
        pair_all,
        after_start,
        current,
        normed,
        left,
        right,
        key_all,
        value_all,
        chain_wide,
        mask_wide,
        start_scores,
        shift,
        own_rows,
        send_first,
        recv_first,
        send_second,
        recv_second,
        load_sem,
    ) = refs[2 * count + 1 :]
    loads = [
        pltpu.make_async_copy(source, target, load_sem.at[index])
        for index, (source, target) in enumerate(zip(sources, held))
    ]
    for load in loads:
        load.start()
    me = lax.axis_index("dap")
    block, width = pair_ref.shape
    length = chain_ref.shape[1]
    mine = block // length
    heads = start_bias_ref.shape[0]
    head_dim = width // heads
    scaling = 1.0 / math.sqrt(head_dim)
    tile = 8
    chunks = length // tile
    chunk_rows = tile * length
    f32, bf16 = jnp.float32, jnp.bfloat16

    barrier = pltpu.get_barrier_semaphore()
    for step in range(1, devices):
        peer = lax.rem(me + step, devices)
        pl.semaphore_signal(
            barrier, inc=1, device_id={"dap": peer}, device_id_type=pl.DeviceIdType.MESH
        )
    pl.semaphore_wait(barrier, devices - 1)

    my_block = pl.ds(pl.multiple_of(me * block, block), block)

    def exchange(source, target, send_sems, recv_sems):
        copies = []
        for step in range(1, devices):
            peer = lax.rem(me + step, devices)
            copies.append(
                pltpu.make_async_remote_copy(
                    src_ref=source,
                    dst_ref=target.at[my_block],
                    send_sem=send_sems.at[step],
                    recv_sem=recv_sems.at[step],
                    device_id={"dap": peer},
                    device_id_type=pl.DeviceIdType.MESH,
                )
            )
        for copy in copies:
            copy.start()
        return copies

    loads[0].wait()
    copies_first = exchange(pair_ref, pair_all, send_first, recv_first)
    pair_all[my_block, :] = pair_ref[...]

    for load in loads[1:]:
        load.wait()

    average = jnp.full((2 * width, width), 1.0 / width, bf16)
    row_head = lax.broadcasted_iota(jnp.int32, (width, width), 0) // head_dim
    lane_head = lax.broadcasted_iota(jnp.int32, (width, width), 1) // head_dim
    same_head = jnp.where(row_head == lane_head, 1.0, 0.0).astype(bf16)
    same_head_twice = jnp.concatenate([same_head, same_head], axis=0)
    spread_heads = jnp.where(
        lax.broadcasted_iota(jnp.int32, (heads, width), 0)
        == lax.broadcasted_iota(jnp.int32, (heads, width), 1) // head_dim,
        1.0,
        0.0,
    ).astype(bf16)
    start_bias_wide = dot_columns(start_bias_ref[...], spread_heads).astype(bf16)
    end_bias_wide = dot_columns(end_bias_ref[...], spread_heads).astype(bf16)
    diagonal = lax.broadcasted_iota(jnp.int32, (length, length), 0) == lax.broadcasted_iota(
        jnp.int32, (length, length), 1
    )
    chain_column = jnp.sum(
        jnp.where(diagonal, chain_ref[...].astype(f32), 0.0), axis=1, keepdims=True
    )
    mask_column = jnp.sum(
        jnp.where(diagonal, mask_ref[...].astype(f32), 0.0), axis=1, keepdims=True
    )
    chain_wide[...] = jnp.broadcast_to(chain_column, (length, width))
    mask_all = jnp.broadcast_to(mask_column, (length, width))
    mask_wide[...] = mask_all
    key_lane = (
        lax.broadcasted_iota(jnp.int32, (length, width), 1) % length
        == lax.broadcasted_iota(jnp.int32, (length, width), 0)
    )
    mask_lanes = jnp.sum(jnp.where(key_lane, mask_all, 0.0), axis=0, keepdims=True)
    key_lane_ones = jnp.where(key_lane, 1.0, 0.0)

    for copy in copies_first:
        copy.wait_recv()

    def sides(chunk, normed_rows, weight_ref):
        projected = dot(normed_rows, weight_ref[...])
        rows_mask = mask_wide[pl.ds(chunk * tile, tile), :]
        pair_mask = jnp.concatenate(
            [mask_all * rows_mask[row : row + 1, :] for row in range(tile)], axis=0
        )
        left_side = pair_mask * sigmoid(projected[:, width : 2 * width]) * projected[:, :width]
        right_side = (
            pair_mask
            * sigmoid(projected[:, 3 * width :])
            * projected[:, 2 * width : 3 * width]
        )
        return left_side.astype(bf16).astype(f32), right_side.astype(bf16).astype(f32)

    def first(chunk, carry):
        rows = pl.ds(pl.multiple_of(chunk * chunk_rows, chunk_rows), chunk_rows)
        chain_rows = chain_wide[pl.ds(chunk * tile, tile), :]
        chain_all = chain_wide[...]
        within = table_ref[1:2, :]
        across = table_ref[0:1, :]
        added = jnp.concatenate(
            [
                jnp.where(chain_all == chain_rows[row : row + 1, :], within, across)
                for row in range(tile)
            ],
            axis=0,
        )
        start = (pair_all[rows, :].astype(f32) + added).astype(bf16)
        current[rows, :] = start
        rows_normed = norm_rows(start, average)
        normed[rows, :] = rows_normed
        left_side, right_side = sides(chunk, rows_normed, out_project_ref)
        left[rows, :] = left_side
        right[rows, :] = right_side
        return carry

    lax.fori_loop(0, chunks, first, 0)

    def finish(rows, combined, gate_ref, final_ref):
        combined_normed = norm_rows(combined.astype(bf16), average)
        update = dot(combined_normed, final_ref[...])
        gate = sigmoid(dot(normed[rows, :], gate_ref[...]))
        return (current[rows, :].astype(f32) + gate * update).astype(bf16)

    def outgoing(chunk, carry):
        rows = pl.ds(pl.multiple_of(chunk * chunk_rows, chunk_rows), chunk_rows)

        def add(step, totals):
            totals = list(totals)
            tiles = [
                left[pl.ds(pl.multiple_of((chunk * tile + row) * length + step * tile, tile), tile), :]
                for row in range(tile)
            ]
            for offset in range(tile):
                others = right[pl.ds(step * tile + offset, length, stride=length), :]
                for row in range(tile):
                    totals[row] = totals[row] + tiles[row][offset : offset + 1, :] * others
            return tuple(totals)

        totals = lax.fori_loop(
            0, chunks, add, tuple(jnp.zeros((length, width), f32) for _ in range(tile))
        )
        combined = jnp.concatenate(totals, axis=0)
        updated = finish(rows, combined, out_gate_ref, out_final_ref)
        current[rows, :] = updated
        return carry

    lax.fori_loop(0, chunks, outgoing, 0)

    def second(chunk, carry):
        rows = pl.ds(pl.multiple_of(chunk * chunk_rows, chunk_rows), chunk_rows)
        rows_normed = norm_rows(current[rows, :], average)
        normed[rows, :] = rows_normed
        left_side, right_side = sides(chunk, rows_normed, in_project_ref)
        left[rows, :] = left_side
        right[rows, :] = right_side
        return carry

    lax.fori_loop(0, chunks, second, 0)

    def incoming(chunk, carry):
        rows = pl.ds(pl.multiple_of(chunk * chunk_rows, chunk_rows), chunk_rows)

        def add(step, totals):
            totals = list(totals)
            for offset in range(tile):
                base = (step * tile + offset) * length
                own = left[pl.ds(pl.multiple_of(base + chunk * tile, tile), tile), :]
                others = right[pl.ds(pl.multiple_of(base, length), length), :]
                for row in range(tile):
                    totals[row] = totals[row] + own[row : row + 1, :] * others
            return tuple(totals)

        totals = lax.fori_loop(
            0, chunks, add, tuple(jnp.zeros((length, width), f32) for _ in range(tile))
        )
        combined = jnp.concatenate(totals, axis=0)
        updated = finish(rows, combined, in_gate_ref, in_final_ref)
        current[rows, :] = updated
        rows_normed = norm_rows(updated, average)
        bias = dot(rows_normed, start_bias_wide)
        bias = jnp.concatenate(
            [
                jnp.sum(
                    bias[row * length : (row + 1) * length, :] * key_lane_ones,
                    axis=0,
                    keepdims=True,
                )
                for row in range(tile)
            ],
            axis=0,
        )
        start_scores[pl.ds(pl.multiple_of(chunk * tile, tile), tile), :] = bias.astype(
            bf16
        ).astype(f32)
        return carry

    lax.fori_loop(0, chunks, incoming, 0)

    before = current[my_block, :]
    projected = dot(norm_rows(before, average), start_project_ref[...])
    gates = sigmoid(projected[:, 3 * width :])
    shared = start_scores[...] + (mask_lanes - 1.0) * mask_scale
    lane_of_head = lax.broadcasted_iota(jnp.int32, (length, width), 1) // length
    attended = []
    for row in range(mine):
        rows = slice(row * length, (row + 1) * length)
        queries = projected[rows, :width].astype(bf16)
        keys = projected[rows, width : 2 * width].astype(bf16)
        values = projected[rows, 2 * width : 3 * width].astype(bf16)
        keys = jnp.concatenate([keys] * heads, axis=0) * same_head
        values = jnp.concatenate([values] * heads, axis=0) * same_head
        scores = dot_rows(queries, keys) * scaling + shared
        top = jnp.zeros_like(scores)
        for head in range(heads):
            own_lanes = lane_of_head == head
            peak = jnp.max(jnp.where(own_lanes, scores, -jnp.inf), axis=1, keepdims=True)
            top = jnp.where(own_lanes, peak, top)
        weights = jnp.exp(scores - top)
        total = dot(halves(weights), same_head_twice)
        weights = (weights / total).astype(bf16)
        attended.append((dot(weights, values) * gates[rows, :]).astype(bf16))
    update = dot(jnp.concatenate(attended, axis=0), start_final_ref[...])
    own_rows[...] = (before.astype(f32) + update).astype(bf16)

    copies_second = exchange(own_rows, after_start, send_second, recv_second)
    own = own_rows[...]
    after_start[my_block, :] = own
    own_projected = dot(norm_rows(own, average), end_project_ref[...])
    for copy in copies_second:
        copy.wait_recv()

    def columns(chunk, carry):
        rows = pl.ds(pl.multiple_of(chunk * chunk_rows, chunk_rows), chunk_rows)
        rows_normed = norm_rows(after_start[rows, :], average)
        projected = dot(rows_normed, end_project_ref[:, width : 3 * width])
        key_all[rows, :] = projected[:, :width].astype(bf16).astype(f32)
        value_all[rows, :] = projected[:, width:].astype(bf16).astype(f32)
        left[rows, :] = dot(rows_normed, end_bias_wide).astype(bf16).astype(f32)
        return carry

    lax.fori_loop(0, chunks, columns, 0)
    gates = sigmoid(own_projected[:, 3 * width :])
    attended = []
    for row in range(mine):
        rows = slice(row * length, (row + 1) * length)
        queries = own_projected[rows, :width].astype(bf16).astype(f32)
        shared = left[pl.ds(me * mine + row, length, stride=length), :] + (
            mask_all - 1.0
        ) * mask_scale
        shift[...] = shared
        queries = jnp.concatenate([queries] * tile, axis=0)

        def score(step, top):
            rows = pl.ds(pl.multiple_of(step * chunk_rows, chunk_rows), chunk_rows)
            products = queries * key_all[rows, :]
            scores = dot(halves(products), same_head_twice) * scaling
            shifts = shift[pl.ds(pl.multiple_of(step * tile, tile), tile), :]
            for part in range(tile):
                piece = scores[part * length : (part + 1) * length, :] + shifts[part : part + 1, :]
                top = jnp.maximum(top, piece)
                right[
                    pl.ds(pl.multiple_of(step * chunk_rows + part * length, length), length), :
                ] = piece
            return top

        top = lax.fori_loop(0, chunks, score, jnp.full((length, width), -jnp.inf, f32))

        def mix(step, totals):
            total, mixed = totals
            for part in range(tile):
                rows = pl.ds(pl.multiple_of(step * chunk_rows + part * length, length), length)
                weights = jnp.exp(right[rows, :] - top)
                total = total + weights
                mixed = mixed + weights * value_all[rows, :]
            return total, mixed

        zero = jnp.zeros((length, width), f32)
        total, mixed = lax.fori_loop(0, chunks, mix, (zero, zero))
        attended.append((mixed / total * gates[slice(row * length, (row + 1) * length), :]).astype(bf16))
    update = dot(jnp.concatenate(attended, axis=0), end_final_ref[...]).astype(bf16)
    after_end = (own.astype(f32) + update.astype(f32)).astype(bf16)

    hidden = dot(norm_rows(after_end, average), trans_up_ref[...])
    hidden = jnp.maximum(hidden, 0.0).astype(bf16)
    update = dot(hidden, trans_down_ref[...])
    result_ref[...] = (after_end.astype(f32) + update).astype(bf16)

    for copy in copies_first + copies_second:
        copy.wait_send()


def fused(devices, pair_act, chain_id, pad_mask, *weights):
    mine, length, width = pair_act.shape
    block = mine * length
    pairs = length * length
    bf16, f32 = jnp.bfloat16, jnp.float32
    start_bias, end_bias = weights[8], weights[11]
    operands = (
        pair_act.reshape(block, width),
        chain_id.reshape(1, length),
        pad_mask.reshape(1, length),
        *weights[:8],
        start_bias.T,
        *weights[9:11],
        end_bias.T,
        *weights[12:],
    )
    count = len(operands)
    result = pl.pallas_call(
        functools.partial(fused_kernel, devices, count),
        out_shape=jax.ShapeDtypeStruct((block, width), bf16),
        in_specs=[pl.BlockSpec(memory_space=pltpu.HBM)] * count,
        out_specs=pl.BlockSpec(memory_space=pltpu.VMEM),
        scratch_shapes=[pltpu.VMEM(operand.shape, operand.dtype) for operand in operands]
        + [
            pltpu.VMEM((pairs, width), bf16),
            pltpu.VMEM((pairs, width), bf16),
            pltpu.VMEM((pairs, width), bf16),
            pltpu.VMEM((pairs, width), bf16),
            pltpu.VMEM((pairs, width), f32),
            pltpu.VMEM((pairs, width), f32),
            pltpu.VMEM((pairs, width), f32),
            pltpu.VMEM((pairs, width), f32),
            pltpu.VMEM((length, width), f32),
            pltpu.VMEM((length, width), f32),
            pltpu.VMEM((length, width), f32),
            pltpu.VMEM((length, width), f32),
            pltpu.VMEM((block, width), bf16),
            pltpu.SemaphoreType.DMA((devices,)),
            pltpu.SemaphoreType.DMA((devices,)),
            pltpu.SemaphoreType.DMA((devices,)),
            pltpu.SemaphoreType.DMA((devices,)),
            pltpu.SemaphoreType.DMA((count,)),
        ],
        compiler_params=pltpu.CompilerParams(
            collective_id=0, has_side_effects=True, vmem_limit_bytes=60 * 1024 * 1024
        ),
    )(*operands)
    return result.reshape(mine, length, width)


def solution(mesh):
    devices = mesh.shape["dap"]

    def per_device(pair_act, chain_id, pad_mask, chain_table, *weights):
        mine, length, width = pair_act.shape
        heads = weights[7].shape[1]
        fits = (
            heads * length == width
            and width // heads == length
            and mine * devices == length
            and (mine * length) % 16 == 0
        )
        if fits:
            return fused(devices, pair_act, chain_id, pad_mask, chain_table, *weights)
        return local(pair_act, chain_id, pad_mask, chain_table, *weights)

    return jax.shard_map(
        per_device,
        mesh=mesh,
        in_specs=(
            P(("groups", "dap"), None, None),
            P("groups"),
            P("groups"),
            P(),
            P(),
            P(),
            P(),
            P(),
            P(),
            P(),
            P(),
            P(),
            P(),
            P(),
            P(),
            P(),
            P(),
            P(),
        ),
        out_specs=P(("groups", "dap"), None, None),
        check_vma=False,
    )
```

```python
import functools
import math

import jax
import jax.numpy as jnp
from jax import lax
from jax.experimental import pallas as pl
from jax.experimental.pallas import tpu as pltpu
from jax.sharding import PartitionSpec as P

epsilon = 1e-05
mask_scale = 1000000000.0


def layer_norm(values, along_axis):
    values = values.astype(jnp.float32)
    centred = values - jnp.mean(values, axis=along_axis, keepdims=True)
    spread = jnp.mean(centred * centred, axis=along_axis, keepdims=True)
    return centred * lax.rsqrt(spread + epsilon)


def regroup_second(values):
    return lax.all_to_all(values, "dap", split_axis=1, concat_axis=0, tiled=True)


def return_columns(values):
    return lax.all_to_all(values, "dap", split_axis=0, concat_axis=1, tiled=True)


def softmax_rows(scores):
    scores = scores - jnp.max(scores, axis=-1, keepdims=True)
    expsum = jnp.exp(scores)
    return (expsum / jnp.sum(expsum, axis=-1, keepdims=True)).astype(jnp.bfloat16)


def triangle_product(
    current, mask_rows, mask_all, weight_project, weight_gate, weight_final, outgoing
):
    hidden_width = weight_project.shape[1] // 4
    normed = layer_norm(current, -1).astype(jnp.bfloat16)
    projected = jnp.einsum(
        "ilc,ce->eil", normed, weight_project, preferred_element_type=jnp.float32
    )
    pair_mask = mask_rows[:, None] * mask_all[None, :]
    left_side = (
        pair_mask
        * jax.nn.sigmoid(projected[hidden_width : 2 * hidden_width])
        * projected[:hidden_width]
    ).astype(jnp.bfloat16)
    right_side = (
        pair_mask
        * jax.nn.sigmoid(projected[3 * hidden_width :])
        * projected[2 * hidden_width : 3 * hidden_width]
    ).astype(jnp.bfloat16)
    left_all, right_all = (
        lax.all_to_all(left_side, "dap", split_axis=0, concat_axis=1, tiled=True),
        lax.all_to_all(right_side, "dap", split_axis=0, concat_axis=1, tiled=True),
    )
    if outgoing:
        combined = jnp.einsum(
            "cik,cjk->cij", left_all, right_all, preferred_element_type=jnp.float32
        )
    else:
        combined = jnp.einsum(
            "cki,ckj->cij", left_all, right_all, preferred_element_type=jnp.float32
        )
    gathered = regroup_second(combined.astype(jnp.bfloat16))
    normed_out = layer_norm(gathered, 0).astype(jnp.bfloat16)
    update = jnp.einsum("cil,cd->ild", normed_out, weight_final, preferred_element_type=jnp.float32)
    gate_full = jax.nn.sigmoid(
        jnp.einsum("ilc,cd->ild", normed, weight_gate, preferred_element_type=jnp.float32)
    )
    return (current.astype(jnp.float32) + gate_full * update).astype(jnp.bfloat16)


def starting_node(current, mask_bias, weight_project, weight_bias, weight_final):
    row_count, length, width = current.shape
    heads = weight_bias.shape[1]
    head_dim = width // heads
    scaling = 1.0 / math.sqrt(head_dim)
    normed = layer_norm(current, -1).astype(jnp.bfloat16)
    projected = jnp.einsum(
        "ijc,ce->ije", normed, weight_project, preferred_element_type=jnp.float32
    )
    queries = (
        projected[..., :width].astype(jnp.bfloat16).reshape(row_count, length, heads, head_dim)
    )
    key_rows = (
        projected[..., width : 2 * width]
        .astype(jnp.bfloat16)
        .reshape(row_count, length, heads, head_dim)
    )
    value_rows = (
        projected[..., 2 * width : 3 * width]
        .astype(jnp.bfloat16)
        .reshape(row_count, length, heads, head_dim)
    )
    gate_values = jax.nn.sigmoid(projected[..., 3 * width :])
    bias_rows = jnp.einsum(
        "jkc,ch->jhk", normed, weight_bias, preferred_element_type=jnp.float32
    ).astype(jnp.bfloat16)
    piece_bias = lax.all_gather(bias_rows, "dap", axis=0, tiled=True)
    piece_rows = piece_bias.shape[0]
    block_rows = math.gcd(piece_rows, 64)

    def per_one_block(block_index):
        offset = block_index * block_rows
        bias_block = lax.dynamic_slice_in_dim(piece_bias, offset, block_rows, 0).astype(jnp.float32)
        query_block = lax.dynamic_slice_in_dim(queries, offset, block_rows, 1)
        scores = (
            jnp.einsum("ijhd,ikhd->ihjk", query_block, key_rows, preferred_element_type=jnp.float32)
            * scaling
        )
        scores = (
            scores + jnp.transpose(bias_block, (1, 0, 2))[None] + mask_bias[None, None, None, :]
        )
        weights = softmax_rows(scores)
        mixed_values = jnp.einsum(
            "ihjk,ikhd->ijhd", weights, value_rows, preferred_element_type=jnp.float32
        )
        mixed_values = mixed_values.reshape(row_count, block_rows, width)
        gate_block = lax.dynamic_slice_in_dim(gate_values, offset, block_rows, 1)
        return (mixed_values * gate_block).astype(jnp.bfloat16)

    blocks = lax.map(per_one_block, jnp.arange(piece_rows // block_rows, dtype=jnp.int32))
    attended = jnp.transpose(blocks, (1, 0, 2, 3)).reshape(row_count, piece_rows, width)
    update = jnp.einsum("ijc,cd->ijd", attended, weight_final, preferred_element_type=jnp.float32)
    return (current.astype(jnp.float32) + update).astype(jnp.bfloat16)


def transition(current, trans_up, trans_down):
    normed = layer_norm(current, -1).astype(jnp.bfloat16)
    hidden = jax.nn.relu(
        jnp.einsum("ijc,cf->ijf", normed, trans_up, preferred_element_type=jnp.float32)
    ).astype(jnp.bfloat16)
    update = jnp.einsum("ijf,fc->ijc", hidden, trans_down, preferred_element_type=jnp.float32)
    return (current.astype(jnp.float32) + update).astype(jnp.bfloat16)


def ending_node(
    current, mask_bias, weight_project, weight_bias, weight_final, trans_up, trans_down
):
    columns = regroup_second(current)
    length, col_count, width = columns.shape
    heads = weight_bias.shape[1]
    head_dim = width // heads
    scaling = 1.0 / math.sqrt(head_dim)
    normed = layer_norm(columns, -1).astype(jnp.bfloat16)
    projected = jnp.einsum(
        "ijc,ce->ije", normed, weight_project, preferred_element_type=jnp.float32
    )
    queries = (
        projected[..., :width].astype(jnp.bfloat16).reshape(length, col_count, heads, head_dim)
    )
    key_cols = (
        projected[..., width : 2 * width]
        .astype(jnp.bfloat16)
        .reshape(length, col_count, heads, head_dim)
    )
    value_cols = (
        projected[..., 2 * width : 3 * width]
        .astype(jnp.bfloat16)
        .reshape(length, col_count, heads, head_dim)
    )
    gate_values = jax.nn.sigmoid(projected[..., 3 * width :])
    own_normed = layer_norm(current, -1).astype(jnp.bfloat16)
    bias_part = jnp.einsum(
        "kic,ch->khi", own_normed, weight_bias, preferred_element_type=jnp.float32
    ).astype(jnp.bfloat16)

    def bias_slice(gathered, offset, block_rows):
        return jnp.transpose(lax.dynamic_slice_in_dim(gathered, offset, block_rows, 2), (1, 2, 0))

    gathered = lax.all_gather(bias_part, "dap", axis=0, tiled=True)
    block_rows = math.gcd(length, 64)

    def ending_one_block(block_index):
        offset = block_index * block_rows
        query_block = lax.dynamic_slice_in_dim(queries, offset, block_rows, 0)
        scores = (
            jnp.einsum("ijhd,kjhd->jhik", query_block, key_cols, preferred_element_type=jnp.float32)
            * scaling
        )
        scores = (
            scores
            + bias_slice(gathered, offset, block_rows).astype(jnp.float32)[None]
            + mask_bias[None, None, None, :]
        )
        weights = softmax_rows(scores)
        mixed_values = jnp.einsum(
            "jhik,kjhd->ijhd", weights, value_cols, preferred_element_type=jnp.float32
        )
        mixed_values = mixed_values.reshape(block_rows, col_count, width)
        gate_block = lax.dynamic_slice_in_dim(gate_values, offset, block_rows, 0)
        return (mixed_values * gate_block).astype(jnp.bfloat16)

    blocks = lax.map(ending_one_block, jnp.arange(length // block_rows, dtype=jnp.int32))
    attended = blocks.reshape(length, col_count, width)
    update = jnp.einsum(
        "ijc,cd->ijd", attended, weight_final, preferred_element_type=jnp.float32
    ).astype(jnp.bfloat16)
    columns = (columns.astype(jnp.float32) + update.astype(jnp.float32)).astype(jnp.bfloat16)
    finished = return_columns(transition(columns, trans_up, trans_down))
    return finished


def local(
    pair_act,
    chain_id,
    pad_mask,
    chain_table,
    out_project,
    out_gate,
    out_final,
    in_project,
    in_gate,
    in_final,
    start_project,
    start_bias,
    start_final,
    end_project,
    end_bias,
    end_final,
    trans_up,
    trans_down,
):
    row_count = pair_act.shape[0]
    first_row = lax.axis_index("dap") * row_count
    mask_all = pad_mask.astype(jnp.float32)
    mask_rows = lax.dynamic_slice_in_dim(mask_all, first_row, row_count, 0)
    chain_rows = lax.dynamic_slice_in_dim(chain_id, first_row, row_count, 0)
    same_chain = chain_rows[:, None] == chain_id[None, :]
    chain_add = jnp.where(
        same_chain[:, :, None], chain_table[1][None, None, :], chain_table[0][None, None, :]
    )
    current = (pair_act.astype(jnp.float32) + chain_add).astype(jnp.bfloat16)
    current = triangle_product(current, mask_rows, mask_all, out_project, out_gate, out_final, True)
    current = triangle_product(current, mask_rows, mask_all, in_project, in_gate, in_final, False)
    mask_bias = (mask_all - 1.0) * mask_scale
    current = starting_node(current, mask_bias, start_project, start_bias, start_final)
    return ending_node(current, mask_bias, end_project, end_bias, end_final, trans_up, trans_down)


def dot(left, right):
    return jnp.dot(left, right, preferred_element_type=jnp.float32)


def dot_rows(left, right):
    return lax.dot_general(
        left, right, (((1,), (1,)), ((), ())), preferred_element_type=jnp.float32
    )


def dot_columns(left, right):
    return lax.dot_general(
        left, right, (((0,), (0,)), ((), ())), preferred_element_type=jnp.float32
    )


def halves(values):
    high = values.astype(jnp.bfloat16)
    low = (values - high.astype(jnp.float32)).astype(jnp.bfloat16)
    return jnp.concatenate([high, low], axis=1)


def sigmoid(values):
    return 0.5 * jnp.tanh(0.5 * values) + 0.5


def norm_rows(values, average):
    width = values.shape[1]
    centred = values.astype(jnp.float32) - dot(values, average[:width])
    spread = dot(halves(centred * centred), average)
    return (centred * lax.rsqrt(spread + epsilon)).astype(jnp.bfloat16)


def fused_kernel(
    devices,
    count,
    *refs,
):
    sources, result_ref, held = refs[:count], refs[count], refs[count + 1 : 2 * count + 1]
    (
        pair_ref,
        chain_ref,
        mask_ref,
        table_ref,
        out_project_ref,
        out_gate_ref,
        out_final_ref,
        in_project_ref,
        in_gate_ref,
        in_final_ref,
        start_project_ref,
        start_bias_ref,
        start_final_ref,
        end_project_ref,
        end_bias_ref,
        end_final_ref,
        trans_up_ref,
        trans_down_ref,
    ) = held
    (
        pair_all,
        after_start,
        current,
        normed,
        left,
        right,
        key_all,
        value_all,
        chain_wide,
        mask_wide,
        start_scores,
        shift,
        own_rows,
        send_first,
        recv_first,
        send_second,
        recv_second,
        load_sem,
    ) = refs[2 * count + 1 :]
    loads = [
        pltpu.make_async_copy(source, target, load_sem.at[index])
        for index, (source, target) in enumerate(zip(sources, held))
    ]
    for load in loads:
        load.start()
    me = lax.axis_index("dap")
    block, width = pair_ref.shape
    length = chain_ref.shape[1]
    mine = block // length
    heads = start_bias_ref.shape[0]
    head_dim = width // heads
    scaling = 1.0 / math.sqrt(head_dim)
    tile = 8
    chunks = length // tile
    chunk_rows = tile * length
    f32, bf16 = jnp.float32, jnp.bfloat16

    barrier = pltpu.get_barrier_semaphore()
    for step in range(1, devices):
        peer = lax.rem(me + step, devices)
        pl.semaphore_signal(
            barrier, inc=1, device_id={"dap": peer}, device_id_type=pl.DeviceIdType.MESH
        )
    pl.semaphore_wait(barrier, devices - 1)

    my_block = pl.ds(pl.multiple_of(me * block, block), block)

    def exchange(source, target, send_sems, recv_sems):
        copies = []
        for step in range(1, devices):
            peer = lax.rem(me + step, devices)
            copies.append(
                pltpu.make_async_remote_copy(
                    src_ref=source,
                    dst_ref=target.at[my_block],
                    send_sem=send_sems.at[step],
                    recv_sem=recv_sems.at[step],
                    device_id={"dap": peer},
                    device_id_type=pl.DeviceIdType.MESH,
                )
            )
        for copy in copies:
            copy.start()
        return copies

    loads[0].wait()
    def arrivals(target, send_sems, recv_sems, order):
        together = chunk_rows // block
        place, chunk, bit = me // together, 0, 1
        while bit < chunks:
            has = lax.rem(place // bit, 2)
            chunk = chunk + (1 - has if (order // bit) % 2 else has) * bit
            bit *= 2
        for member in range(1 if order == 0 else 0, together):
            source = chunk * together + lax.rem(me + member, together)
            step = lax.rem(me - source + devices, devices)
            landed = pl.ds(pl.multiple_of(source * block, block), block)
            pltpu.make_async_remote_copy(
                src_ref=target.at[landed],
                dst_ref=target.at[landed],
                send_sem=send_sems.at[step],
                recv_sem=recv_sems.at[step],
                device_id={"dap": source},
                device_id_type=pl.DeviceIdType.MESH,
            ).wait_recv()
        return chunk

    copies_first = exchange(pair_ref, pair_all, send_first, recv_first)
    pair_all[my_block, :] = pair_ref[...]

    for load in loads[1:]:
        load.wait()

    average = jnp.full((2 * width, width), 1.0 / width, bf16)
    row_head = lax.broadcasted_iota(jnp.int32, (width, width), 0) // head_dim
    lane_head = lax.broadcasted_iota(jnp.int32, (width, width), 1) // head_dim
    same_head = jnp.where(row_head == lane_head, 1.0, 0.0).astype(bf16)
    same_head_twice = jnp.concatenate([same_head, same_head], axis=0)
    spread_heads = jnp.where(
        lax.broadcasted_iota(jnp.int32, (heads, width), 0)
        == lax.broadcasted_iota(jnp.int32, (heads, width), 1) // head_dim,
        1.0,
        0.0,
    ).astype(bf16)
    start_bias_wide = dot_columns(start_bias_ref[...], spread_heads).astype(bf16)
    end_bias_wide = dot_columns(end_bias_ref[...], spread_heads).astype(bf16)
    diagonal = lax.broadcasted_iota(jnp.int32, (length, length), 0) == lax.broadcasted_iota(
        jnp.int32, (length, length), 1
    )
    chain_column = jnp.sum(
        jnp.where(diagonal, chain_ref[...].astype(f32), 0.0), axis=1, keepdims=True
    )
    mask_column = jnp.sum(
        jnp.where(diagonal, mask_ref[...].astype(f32), 0.0), axis=1, keepdims=True
    )
    chain_wide[...] = jnp.broadcast_to(chain_column, (length, width))
    mask_all = jnp.broadcast_to(mask_column, (length, width))
    mask_wide[...] = mask_all
    key_lane = (
        lax.broadcasted_iota(jnp.int32, (length, width), 1) % length
        == lax.broadcasted_iota(jnp.int32, (length, width), 0)
    )
    mask_lanes = jnp.sum(jnp.where(key_lane, mask_all, 0.0), axis=0, keepdims=True)
    key_lane_ones = jnp.where(key_lane, 1.0, 0.0)

    def sides(chunk, normed_rows, weight_ref):
        projected = dot(normed_rows, weight_ref[...])
        rows_mask = mask_wide[pl.ds(chunk * tile, tile), :]
        pair_mask = jnp.concatenate(
            [mask_all * rows_mask[row : row + 1, :] for row in range(tile)], axis=0
        )
        left_side = pair_mask * sigmoid(projected[:, width : 2 * width]) * projected[:, :width]
        right_side = (
            pair_mask
            * sigmoid(projected[:, 3 * width :])
            * projected[:, 2 * width : 3 * width]
        )
        return left_side.astype(bf16).astype(f32), right_side.astype(bf16).astype(f32)

    def first(chunk, carry):
        rows = pl.ds(pl.multiple_of(chunk * chunk_rows, chunk_rows), chunk_rows)
        chain_rows = chain_wide[pl.ds(chunk * tile, tile), :]
        chain_all = chain_wide[...]
        within = table_ref[1:2, :]
        across = table_ref[0:1, :]
        added = jnp.concatenate(
            [
                jnp.where(chain_all == chain_rows[row : row + 1, :], within, across)
                for row in range(tile)
            ],
            axis=0,
        )
        start = (pair_all[rows, :].astype(f32) + added).astype(bf16)
        current[rows, :] = start
        rows_normed = norm_rows(start, average)
        normed[rows, :] = rows_normed
        left_side, right_side = sides(chunk, rows_normed, out_project_ref)
        for row in range(tile):
            piece = slice(row * length, (row + 1) * length)
            turned = pl.ds(chunk * tile + row, length, stride=length)
            left[turned, :] = left_side[piece, :]
            right[turned, :] = right_side[piece, :]
        return carry

    for order in range(chunks):
        first(arrivals(pair_all, send_first, recv_first, order), 0)

    def finish(rows, combined, gate_ref, final_ref):
        combined_normed = norm_rows(combined.astype(bf16), average)
        update = dot(combined_normed, final_ref[...])
        gate = sigmoid(dot(normed[rows, :], gate_ref[...]))
        return (current[rows, :].astype(f32) + gate * update).astype(bf16)

    def outgoing(chunk, carry):
        rows = pl.ds(pl.multiple_of(chunk * chunk_rows, chunk_rows), chunk_rows)

        def add(step, totals):
            totals = list(totals)
            for offset in range(tile):
                base = (step * tile + offset) * length
                own = left[pl.ds(pl.multiple_of(base + chunk * tile, tile), tile), :]
                others = right[pl.ds(pl.multiple_of(base, length), length), :]
                for row in range(tile):
                    totals[row] = totals[row] + own[row : row + 1, :] * others
            return tuple(totals)

        totals = lax.fori_loop(
            0, chunks, add, tuple(jnp.zeros((length, width), f32) for _ in range(tile)), unroll=True
        )
        combined = jnp.concatenate(totals, axis=0)
        updated = finish(rows, combined, out_gate_ref, out_final_ref)
        current[rows, :] = updated
        return carry

    lax.fori_loop(0, chunks, outgoing, 0, unroll=2)

    def second(chunk, carry):
        rows = pl.ds(pl.multiple_of(chunk * chunk_rows, chunk_rows), chunk_rows)
        rows_normed = norm_rows(current[rows, :], average)
        normed[rows, :] = rows_normed
        left_side, right_side = sides(chunk, rows_normed, in_project_ref)
        left[rows, :] = left_side
        right[rows, :] = right_side
        return carry

    lax.fori_loop(0, chunks, second, 0, unroll=True)

    def incoming(chunk, carry):
        rows = pl.ds(pl.multiple_of(chunk * chunk_rows, chunk_rows), chunk_rows)

        def add(step, totals):
            totals = list(totals)
            for offset in range(tile):
                base = (step * tile + offset) * length
                own = left[pl.ds(pl.multiple_of(base + chunk * tile, tile), tile), :]
                others = right[pl.ds(pl.multiple_of(base, length), length), :]
                for row in range(tile):
                    totals[row] = totals[row] + own[row : row + 1, :] * others
            return tuple(totals)

        totals = lax.fori_loop(
            0, chunks, add, tuple(jnp.zeros((length, width), f32) for _ in range(tile)), unroll=True
        )
        combined = jnp.concatenate(totals, axis=0)
        updated = finish(rows, combined, in_gate_ref, in_final_ref)
        current[rows, :] = updated
        rows_normed = norm_rows(updated, average)
        bias = dot(rows_normed, start_bias_wide)
        bias = jnp.concatenate(
            [
                jnp.sum(
                    bias[row * length : (row + 1) * length, :] * key_lane_ones,
                    axis=0,
                    keepdims=True,
                )
                for row in range(tile)
            ],
            axis=0,
        )
        start_scores[pl.ds(pl.multiple_of(chunk * tile, tile), tile), :] = bias.astype(
            bf16
        ).astype(f32)
        return carry

    lax.fori_loop(0, chunks, incoming, 0, unroll=2)

    before = current[my_block, :]
    projected = dot(norm_rows(before, average), start_project_ref[...])
    gates = sigmoid(projected[:, 3 * width :])
    shared = start_scores[...] + (mask_lanes - 1.0) * mask_scale
    lane_of_head = lax.broadcasted_iota(jnp.int32, (length, width), 1) // length
    attended = []
    for row in range(mine):
        rows = slice(row * length, (row + 1) * length)
        queries = projected[rows, :width].astype(bf16)
        keys = projected[rows, width : 2 * width].astype(bf16)
        values = projected[rows, 2 * width : 3 * width].astype(bf16)
        keys = jnp.concatenate([keys] * heads, axis=0) * same_head
        values = jnp.concatenate([values] * heads, axis=0) * same_head
        scores = dot_rows(queries, keys) * scaling + shared
        top = jnp.zeros_like(scores)
        for head in range(heads):
            own_lanes = lane_of_head == head
            peak = jnp.max(jnp.where(own_lanes, scores, -jnp.inf), axis=1, keepdims=True)
            top = jnp.where(own_lanes, peak, top)
        weights = jnp.exp(scores - top)
        total = dot(halves(weights), same_head_twice)
        weights = (weights / total).astype(bf16)
        attended.append((dot(weights, values) * gates[rows, :]).astype(bf16))
    update = dot(jnp.concatenate(attended, axis=0), start_final_ref[...])
    own_rows[...] = (before.astype(f32) + update).astype(bf16)

    copies_second = exchange(own_rows, after_start, send_second, recv_second)
    own = own_rows[...]
    after_start[my_block, :] = own
    own_projected = dot(norm_rows(own, average), end_project_ref[...])

    def columns(chunk, carry):
        rows = pl.ds(pl.multiple_of(chunk * chunk_rows, chunk_rows), chunk_rows)
        rows_normed = norm_rows(after_start[rows, :], average)
        projected = dot(rows_normed, end_project_ref[:, width : 3 * width])
        key_all[rows, :] = projected[:, :width].astype(bf16).astype(f32)
        value_all[rows, :] = projected[:, width:].astype(bf16).astype(f32)
        left[rows, :] = dot(rows_normed, end_bias_wide).astype(bf16).astype(f32)
        return carry

    for order in range(chunks):
        columns(arrivals(after_start, send_second, recv_second, order), 0)
    gates = sigmoid(own_projected[:, 3 * width :])
    attended = []
    for row in range(mine):
        rows = slice(row * length, (row + 1) * length)
        queries = own_projected[rows, :width].astype(bf16).astype(f32)
        shared = left[pl.ds(me * mine + row, length, stride=length), :] + (
            mask_all - 1.0
        ) * mask_scale
        shift[...] = shared
        queries = jnp.concatenate([queries] * tile, axis=0)

        def score(step, top):
            rows = pl.ds(pl.multiple_of(step * chunk_rows, chunk_rows), chunk_rows)
            products = queries * key_all[rows, :]
            scores = dot(halves(products), same_head_twice) * scaling
            shifts = shift[pl.ds(pl.multiple_of(step * tile, tile), tile), :]
            for part in range(tile):
                piece = scores[part * length : (part + 1) * length, :] + shifts[part : part + 1, :]
                top = jnp.maximum(top, piece)
                right[
                    pl.ds(pl.multiple_of(step * chunk_rows + part * length, length), length), :
                ] = piece
            return top

        top = lax.fori_loop(0, chunks, score, jnp.full((length, width), -jnp.inf, f32), unroll=True)

        def mix(step, totals):
            total, mixed = totals
            for part in range(tile):
                rows = pl.ds(pl.multiple_of(step * chunk_rows + part * length, length), length)
                weights = jnp.exp(right[rows, :] - top)
                total = total + weights
                mixed = mixed + weights * value_all[rows, :]
            return total, mixed

        zero = jnp.zeros((length, width), f32)
        total, mixed = lax.fori_loop(0, chunks, mix, (zero, zero), unroll=True)
        attended.append((mixed / total * gates[slice(row * length, (row + 1) * length), :]).astype(bf16))
    update = dot(jnp.concatenate(attended, axis=0), end_final_ref[...]).astype(bf16)
    after_end = (own.astype(f32) + update.astype(f32)).astype(bf16)

    hidden = dot(norm_rows(after_end, average), trans_up_ref[...])
    hidden = jnp.maximum(hidden, 0.0).astype(bf16)
    update = dot(hidden, trans_down_ref[...])
    result_ref[...] = (after_end.astype(f32) + update).astype(bf16)

    for copy in copies_first + copies_second:
        copy.wait_send()


def fused(devices, pair_act, chain_id, pad_mask, *weights):
    mine, length, width = pair_act.shape
    block = mine * length
    pairs = length * length
    bf16, f32 = jnp.bfloat16, jnp.float32
    start_bias, end_bias = weights[8], weights[11]
    operands = (
        pair_act.reshape(block, width),
        chain_id.reshape(1, length),
        pad_mask.reshape(1, length),
        *weights[:8],
        start_bias.T,
        *weights[9:11],
        end_bias.T,
        *weights[12:],
    )
    count = len(operands)
    result = pl.pallas_call(
        functools.partial(fused_kernel, devices, count),
        out_shape=jax.ShapeDtypeStruct((block, width), bf16),
        in_specs=[pl.BlockSpec(memory_space=pltpu.HBM)] * count,
        out_specs=pl.BlockSpec(memory_space=pltpu.VMEM),
        scratch_shapes=[pltpu.VMEM(operand.shape, operand.dtype) for operand in operands]
        + [
            pltpu.VMEM((pairs, width), bf16),
            pltpu.VMEM((pairs, width), bf16),
            pltpu.VMEM((pairs, width), bf16),
            pltpu.VMEM((pairs, width), bf16),
            pltpu.VMEM((pairs, width), f32),
            pltpu.VMEM((pairs, width), f32),
            pltpu.VMEM((pairs, width), f32),
            pltpu.VMEM((pairs, width), f32),
            pltpu.VMEM((length, width), f32),
            pltpu.VMEM((length, width), f32),
            pltpu.VMEM((length, width), f32),
            pltpu.VMEM((length, width), f32),
            pltpu.VMEM((block, width), bf16),
            pltpu.SemaphoreType.DMA((devices,)),
            pltpu.SemaphoreType.DMA((devices,)),
            pltpu.SemaphoreType.DMA((devices,)),
            pltpu.SemaphoreType.DMA((devices,)),
            pltpu.SemaphoreType.DMA((count,)),
        ],
        compiler_params=pltpu.CompilerParams(
            collective_id=0, has_side_effects=True, vmem_limit_bytes=60 * 1024 * 1024
        ),
    )(*operands)
    return result.reshape(mine, length, width)


def solution(mesh):
    devices = mesh.shape["dap"]

    def per_device(pair_act, chain_id, pad_mask, chain_table, *weights):
        mine, length, width = pair_act.shape
        heads = weights[7].shape[1]
        fits = (
            heads * length == width
            and width // heads == length
            and mine * devices == length
            and 8 % mine == 0
            and length % 8 == 0
            and (length // 8) & (length // 8 - 1) == 0
            and (mine * length) % 16 == 0
        )
        if fits:
            return fused(devices, pair_act, chain_id, pad_mask, chain_table, *weights)
        return local(pair_act, chain_id, pad_mask, chain_table, *weights)

    return jax.shard_map(
        per_device,
        mesh=mesh,
        in_specs=(
            P(("groups", "dap"), None, None),
            P("groups"),
            P("groups"),
            P(),
            P(),
            P(),
            P(),
            P(),
            P(),
            P(),
            P(),
            P(),
            P(),
            P(),
            P(),
            P(),
            P(),
            P(),
        ),
        out_specs=P(("groups", "dap"), None, None),
        check_vma=False,
    )
```
